32 devices in a mesh: parts: 2 (over y), tensor: 4 (over z), section: 2 (over x), rows: 2 (over core).
Axes of the slice: x: 2, y: 2, z: 4, core: 2. Of those that a mesh axis runs over, the one named last changes fastest.
Arguments:
- tokens: bfloat16 [96, 8192], P('parts', ('tensor', 'rows')), parts along dimension 0, may hold values from -6 to 6
- gain: float32 [2, 8192], P('section'), may hold values from 0.1 to 1.9
- base_weight: bfloat16 [2, 8192, 8192], P('section', None, ('tensor', 'rows')), may hold values from -0.0625 to 0.0625
- down_weight_slots: bfloat16 [2, 4, 32, 8192], P('section', 'tensor', None, 'rows'), may hold values from -0.0625 to 0.0625
- up_weight_slots: bfloat16 [2, 4, 32, 8192], P('section', 'tensor', None, 'rows'), may hold values from -1 to 1
- row_adapter_index: int32 [96], P('parts'), parts along dimension 0, may hold values from 0 to 3
- adapter_slot_index: int32 [4], replicated, may hold values from 0 to 3, each once
Outputs:
- mixed: bfloat16 [96, 8192], P(('parts', 'section'), ('tensor', 'rows')), parts along dimension 0
The draws below stay inside these ranges and needn't reach their ends.
There are 2 independent parts, one for each index of `parts`. The reference program is written for one: setup_inputs(seed, part) draws one part's arguments, and reference() takes and returns one part's arrays. A program takes and returns all parts, laid end to end along the dimension named above; an argument that names none is the same for every part. Nothing has to cross between parts.
Inputs may be any that keep to these rules, and one draw needn't show every extreme that they name: `adapter_slot_index`: each adapter's storage slot; every slot is used once.
All inputs are finite; a program needn't handle non-finite values.
Results may differ from the reference program's by a relative error of at most 0.0059.
Values may be sent and summed in bfloat16 or wider, within the bound.
A program may use at most 64 MiB of HBM per device.

```python
import math
import jax
import jax.numpy as jnp
import numpy as np
from jax import lax

MODEL_WIDTH = 8192
ADAPTER_RANK = 32
TOKENS = 48
LAYER_COUNT = 2
ADAPTER_COUNT = 4


def plant(drawn, stream_key, smallest, largest):
    spot = [jax.random.randint(jax.random.fold_in(stream_key, axis), (), 0, length) for axis, length in enumerate(drawn.shape)]
    widest = drawn.shape.index(max(drawn.shape))
    next_to = spot[:widest] + [(spot[widest] + 1) % drawn.shape[widest]] + spot[widest + 1:]
    return drawn.at[tuple(spot)].set(smallest).at[tuple(next_to)].set(largest)


def steps_of(rng, dims, pieces, low, high):
    def one(position, blocks):
        steps = jax.random.uniform(jax.random.fold_in(jax.random.fold_in(rng, 6), position), (blocks,), jnp.float32, low / len(pieces), high / len(pieces))
        return jnp.repeat(jnp.exp(steps), dims[position] // blocks).reshape((-1,) + (1,) * (len(dims) - position - 1))

    loudness = one(*pieces[0])
    for cut in pieces[1:]:
        loudness = loudness * one(*cut)
    return loudness


def rank_table(count, slope):
    portions = [(1 << 20) // math.isqrt(grade ** slope) + 1 for grade in range(1, count + 1)]
    width = 1 + sum(portions) // (1 << 30)
    return np.cumsum(np.array([max(1, weight // width) for weight in portions]))


def ranked(stream_key, dims, number_of, skew):
    table = rank_table(number_of, skew)
    ticket = jax.random.randint(jax.random.fold_in(stream_key, 1), dims, 0, int(table[number_of - 1]))
    rank = jnp.searchsorted(jnp.asarray(table, jnp.int32), ticket, side="right")
    return jax.random.permutation(jax.random.fold_in(stream_key, 2), number_of)[rank].astype(jnp.int32)


def normal_values(stream_key, dims, spread, limit, split=(), kind=jnp.bfloat16):
    entries = jax.random.normal(stream_key, dims, jnp.float32) * spread
    if len(split) > 0:
        entries = steps_of(stream_key, dims, split, -0.22, 0.18) * entries
    return jnp.clip(entries, min=-limit, max=limit).astype(kind)


def setup_inputs(seed: int = 0, part: int = 0) -> dict:
    key_of = jax.random.split(jax.random.key(seed), 8)
    own_keys = jax.random.split(jax.random.fold_in(key_of[7], part), 8)
    tokens = normal_values(own_keys[0], (TOKENS, MODEL_WIDTH), 1.0, 6.0, ((1, 8),))
    gain = jnp.clip(1.0 + 0.18 * jax.random.normal(key_of[1], (LAYER_COUNT, MODEL_WIDTH), jnp.float32), 0.1, 1.9)
    base_weight = normal_values(key_of[2], (LAYER_COUNT, MODEL_WIDTH, MODEL_WIDTH), MODEL_WIDTH ** -0.5, 0.0625, ((0, 2), (2, 8)))
    down_weight_slots = normal_values(key_of[3], (LAYER_COUNT, ADAPTER_COUNT, ADAPTER_RANK, MODEL_WIDTH), MODEL_WIDTH ** -0.5, 0.0625, ((0, 2), (1, 4), (3, 2)))
    up_weight_slots = normal_values(key_of[4], (LAYER_COUNT, ADAPTER_COUNT, ADAPTER_RANK, MODEL_WIDTH), ADAPTER_RANK ** -0.5, 1.0, ((0, 2), (1, 4), (3, 2)))
    row_adapter_index = plant(ranked(own_keys[5], (TOKENS,), ADAPTER_COUNT, 2), jax.random.fold_in(own_keys[5], 3), 0, ADAPTER_COUNT - 1).astype(jnp.int32)
    adapter_slot_index = jax.random.permutation(key_of[6], ADAPTER_COUNT).astype(jnp.int32)
    return {"tokens": tokens, "gain": gain, "base_weight": base_weight, "down_weight_slots": down_weight_slots, "up_weight_slots": up_weight_slots, "row_adapter_index": row_adapter_index, "adapter_slot_index": adapter_slot_index}


epsilon = 1e-05

def reference(tokens, gain, base_weight, down_weight_slots, up_weight_slots, row_adapter_index, adapter_slot_index):
    slot_rows = adapter_slot_index[row_adapter_index].astype(jnp.int32)
    slot_hot = (slot_rows[:, None] == jnp.arange(ADAPTER_COUNT, dtype=jnp.int32)[None, :]).astype(jnp.float32)
    hidden = tokens
    for layer_number in range(LAYER_COUNT):
        values = hidden.astype(jnp.float32)
        mean_square = lax.optimization_barrier(jnp.mean(values * values, axis=1, keepdims=True))
        normalized_input = (values * gain[layer_number] * lax.rsqrt(mean_square + epsilon)).astype(jnp.bfloat16)
        projected = jnp.dot(normalized_input, base_weight[layer_number], preferred_element_type=jnp.float32)
        rank_scores = jnp.einsum('be,cqe->bcq', normalized_input.astype(jnp.float32), down_weight_slots[layer_number].astype(jnp.float32))
        lowrank = lax.optimization_barrier(jnp.sum(rank_scores * slot_hot[:, :, None], axis=1)).astype(jnp.bfloat16)
        expanded_update = (slot_hot[:, :, None] * lowrank.astype(jnp.float32)[:, None, :]).astype(jnp.bfloat16)
        adapter_update = jnp.einsum('iqw,qwx->ix', expanded_update.astype(jnp.float32), up_weight_slots[layer_number].astype(jnp.float32))
        hidden = (values + projected + 0.5 * adapter_update).astype(jnp.bfloat16)
    return hidden
```

```python
import functools

import jax
import jax.numpy as jnp
from jax import lax
from jax.experimental import pallas as pl
from jax.experimental.pallas import tpu as pltpu
from jax.sharding import PartitionSpec as P

MESH = pl.DeviceIdType.MESH
epsilon = 1e-05
column_tile = 256


def crossed(position, offset, count):
    result = position
    bit = 1
    while bit < count:
        if offset & bit:
            result = result + bit - 2 * bit * lax.rem(lax.div(position, bit), 2)
        bit *= 2
    return result


def kernel(
    sections,
    tensors,
    tokens_ref,
    gain_ref,
    weight_ref,
    down_ref,
    up_ref,
    row_ref,
    slot_ref,
    out_ref,
    x_buf,
    w_buf,
    gain_buf,
    down_buf,
    up_buf,
    acc,
    normed,
    score,
    score_sib,
    low_buf,
    chain_buf,
    out_buf,
    token_sem,
    gain_sem,
    down_sem,
    w_sem,
    x_send,
    x_recv,
    fwd_send,
    fwd_recv,
    up_send,
    up_recv,
    up_local,
    score_send,
    score_recv,
    low_send,
    low_recv,
    chain_send,
    chain_recv,
    out_send,
    out_recv,
    out_local,
):
    s = lax.axis_index("section")
    t = lax.axis_index("tensor")
    h = lax.axis_index("rows")
    other = 1 - h
    rows, width = x_buf.shape[2], x_buf.shape[3]
    rank = down_buf.shape[0]
    me = t * 2 + h
    peers = [crossed(t, j, tensors) for j in range(tensors)]

    def block_of(j, hh):
        return peers[j] * 2 + (h if hh == 0 else other)

    token_copy = pltpu.make_async_copy(tokens_ref, x_buf.at[0, 0], token_sem)

    @pl.when(s == 0)
    def _():
        token_copy.start()

    gain_copy = pltpu.make_async_copy(gain_ref, gain_buf, gain_sem)
    gain_copy.start()
    down_copy = pltpu.make_async_copy(down_ref.at[0, 0], down_buf, down_sem)
    down_copy.start()

    def w_copy(j, hh):
        first = pl.multiple_of(block_of(j, hh) * width, width)
        return pltpu.make_async_copy(
            weight_ref.at[0, pl.ds(first, width), :], w_buf.at[j, hh], w_sem.at[j, hh]
        )

    for j in range(tensors):
        for hh in range(2):
            w_copy(j, hh).start()

    barrier = pltpu.get_barrier_semaphore()
    for j in range(tensors):
        for hh in range(2):
            if j or hh:
                pl.semaphore_signal(
                    barrier,
                    inc=1,
                    device_id={"tensor": peers[j], "rows": h if hh == 0 else other},
                    device_id_type=MESH,
                )
    for step in range(1, sections):
        pl.semaphore_signal(
            barrier,
            inc=1,
            device_id={"section": lax.rem(s + step, sections)},
            device_id_type=MESH,
        )
    pl.semaphore_wait(barrier, 2 * tensors - 1 + sections - 1)

    def up_remote(i):
        dest = h * tensors + i
        return pltpu.make_async_remote_copy(
            src_ref=up_ref.at[0, 0, :, pl.ds(i * width, width)],
            dst_ref=up_buf.at[t],
            send_sem=up_send.at[i],
            recv_sem=up_recv.at[t],
            device_id={"tensor": lax.div(dest, 2), "rows": lax.rem(dest, 2)},
            device_id_type=MESH,
        )

    def up_here(i):
        return pltpu.make_async_copy(
            up_ref.at[0, 0, :, pl.ds(i * width, width)], up_buf.at[t], up_local
        )

    def send_up():
        for i in range(tensors):

            @pl.when(h * tensors + i != me)
            def _():
                up_remote(i).start()

            @pl.when(h * tensors + i == me)
            def _():
                up_here(i).start()

    def chain():
        return pltpu.make_async_remote_copy(
            src_ref=chain_buf,
            dst_ref=x_buf.at[0, 0],
            send_sem=chain_send,
            recv_sem=chain_recv,
            device_id={"section": lax.rem(s + 1, sections)},
            device_id_type=MESH,
        )

    def x_copy(j):
        return pltpu.make_async_remote_copy(
            src_ref=x_buf.at[0, 0],
            dst_ref=x_buf.at[j, 0],
            send_sem=x_send.at[j],
            recv_sem=x_recv.at[j],
            device_id={"tensor": peers[j]},
            device_id_type=MESH,
        )

    def fwd_copy(j):
        return pltpu.make_async_remote_copy(
            src_ref=x_buf.at[j, 0],
            dst_ref=x_buf.at[j, 1],
            send_sem=fwd_send.at[j],
            recv_sem=fwd_recv.at[j],
            device_id={"rows": other},
            device_id_type=MESH,
        )

    @pl.when(s > 0)
    def _():
        send_up()
        chain().wait_recv()

    @pl.when(s == 0)
    def _():
        token_copy.wait()

    for j in range(1, tensors):
        x_copy(j).start()
    fwd_copy(0).start()

    @pl.when(s == 0)
    def _():
        send_up()

    row = row_ref[...]
    slot_row = jnp.zeros_like(row)
    for a in range(slot_ref.shape[1]):
        slot_row = jnp.where(row == a, slot_ref[0, a], slot_row)
    grid_shape = (rows, rows)
    diagonal = lax.broadcasted_iota(jnp.int32, grid_shape, 0) == lax.broadcasted_iota(
        jnp.int32, grid_shape, 1
    )
    spread = jnp.broadcast_to(slot_row.astype(jnp.float32), grid_shape)
    slot_column = jnp.sum(jnp.where(diagonal, spread, 0.0), axis=1, keepdims=True)
    hot_here = (slot_column == t.astype(jnp.float32)).astype(jnp.float32)

    gain_copy.wait()
    down_copy.wait()
    score[...] = jnp.zeros_like(score)
    squares = jnp.zeros((rows, 1), jnp.float32)
    for j in range(tensors):
        for hh in range(2):
            if hh == 0 and j > 0:
                x_copy(j).wait_recv()
                fwd_copy(j).start()
            if hh == 1:
                fwd_copy(j).wait_recv()
            block = block_of(j, hh)
            values = x_buf[j, hh].astype(jnp.float32)
            squares = squares + jnp.sum(values * values, axis=1, keepdims=True)
            gains = gain_buf[:, pl.ds(pl.multiple_of(block * width, width), width)]
            normed[...] = (values * gains).astype(jnp.bfloat16)
            w_copy(j, hh).wait()
            first = j == 0 and hh == 0

            @pl.loop(0, width // column_tile)
            def _(n):
                columns = pl.ds(pl.multiple_of(n * column_tile, column_tile), column_tile)
                part = jnp.dot(
                    normed[...], w_buf[j, hh, :, columns], preferred_element_type=jnp.float32
                )
                acc[:, columns] = part if first else acc[:, columns] + part

            @pl.when(lax.div(block, tensors) == h)
            def _():
                place = pl.multiple_of((block - h * tensors) * width, width)
                score[...] += lax.dot_general(
                    normed[...],
                    down_buf[:, pl.ds(place, width)],
                    (((1,), (1,)), ((), ())),
                    preferred_element_type=jnp.float32,
                )

    scale = lax.rsqrt(squares / (2 * tensors * width) + epsilon)

    score_copy = pltpu.make_async_remote_copy(
        src_ref=score,
        dst_ref=score_sib,
        send_sem=score_send,
        recv_sem=score_recv,
        device_id={"rows": other},
        device_id_type=MESH,
    )
    score_copy.start()
    score_copy.wait_recv()
    low_buf[0] = (hot_here * (score[...] + score_sib[...]) * scale).astype(jnp.bfloat16)

    def low_copy(j):
        return pltpu.make_async_remote_copy(
            src_ref=low_buf.at[0],
            dst_ref=low_buf.at[j],
            send_sem=low_send.at[j],
            recv_sem=low_recv.at[j],
            device_id={"tensor": peers[j]},
            device_id_type=MESH,
        )

    for j in range(1, tensors):
        low_copy(j).start()

    half_here = lax.div(me, tensors)
    for k in range(tensors):
        local = (t == k) & (h == half_here)

        @pl.when(local)
        def _():
            up_here(0).wait()

        @pl.when(jnp.logical_not(local))
        def _():
            pltpu.make_async_remote_copy(
                src_ref=up_buf.at[k],
                dst_ref=up_buf.at[k],
                send_sem=up_send.at[0],
                recv_sem=up_recv.at[k],
                device_id={"rows": other},
                device_id_type=MESH,
            ).wait_recv()

    total = x_buf[0, 0].astype(jnp.float32) + scale * acc[...]
    for j in range(tensors):
        if j > 0:
            low_copy(j).wait_recv()
        total = total + 0.5 * jnp.dot(
            low_buf[j], up_buf[peers[j]], preferred_element_type=jnp.float32
        )

    @pl.when(s < sections - 1)
    def _():
        chain_buf[...] = total.astype(jnp.bfloat16)
        chain().start()

    share = rows // sections

    def out_copy(d):
        return pltpu.make_async_remote_copy(
            src_ref=out_buf.at[d],
            dst_ref=out_ref,
            send_sem=out_send.at[d],
            recv_sem=out_recv,
            device_id={"section": d},
            device_id_type=MESH,
        )

    @pl.when(s == sections - 1)
    def _():
        for d in range(sections):
            out_buf[d] = total[d * share : (d + 1) * share].astype(jnp.bfloat16)
        here = pltpu.make_async_copy(out_buf.at[sections - 1], out_ref, out_local)
        here.start()
        for d in range(sections - 1):
            out_copy(d).start()
        here.wait()
        for d in range(sections - 1):
            out_copy(d).wait_send()

    for j in range(tensors):
        if j > 0:
            x_copy(j).wait_send()
            low_copy(j).wait_send()
        fwd_copy(j).wait_send()
    score_copy.wait_send()
    for i in range(tensors):

        @pl.when(h * tensors + i != me)
        def _():
            up_remote(i).wait_send()

    @pl.when(s < sections - 1)
    def _():
        chain().wait_send()
        out_copy(0).wait_recv()


def solution(mesh):
    sections, tensors = mesh.shape["section"], mesh.shape["tensor"]

    def shards(tokens, gain, base_weight, down, up, row_adapter, adapter_slot):
        rows, width = tokens.shape
        features = gain.shape[1]
        rank = down.shape[2]
        bf16, f32 = jnp.bfloat16, jnp.float32
        dma = pltpu.SemaphoreType.DMA
        hbm = pl.BlockSpec(memory_space=pl.ANY)
        vmem = pl.BlockSpec(memory_space=pltpu.VMEM)
        smem = pl.BlockSpec(memory_space=pltpu.SMEM)
        return pl.pallas_call(
            functools.partial(kernel, sections, tensors),
            out_shape=jax.ShapeDtypeStruct((rows // sections, width), bf16),
            in_specs=[hbm, hbm, hbm, hbm, hbm, vmem, smem],
            out_specs=hbm,
            scratch_shapes=[
                pltpu.VMEM((tensors, 2, rows, width), bf16),
                pltpu.VMEM((tensors, 2, width, width), bf16),
                pltpu.VMEM((1, features), f32),
                pltpu.VMEM((rank, down.shape[3]), bf16),
                pltpu.VMEM((tensors, rank, width), bf16),
                pltpu.VMEM((rows, width), f32),
                pltpu.VMEM((rows, width), bf16),
                pltpu.VMEM((rows, rank), f32),
                pltpu.VMEM((rows, rank), f32),
                pltpu.VMEM((tensors, rows, rank), bf16),
                pltpu.VMEM((rows, width), bf16),
                pltpu.VMEM((sections, rows // sections, width), bf16),
                dma,
                dma,
                dma,
                dma((tensors, 2)),
                dma((tensors,)),
                dma((tensors,)),
                dma((tensors,)),
                dma((tensors,)),
                dma((tensors,)),
                dma((tensors,)),
                dma,
                dma,
                dma,
                dma((tensors,)),
                dma((tensors,)),
                dma,
                dma,
                dma((sections,)),
                dma,
                dma,
            ],
            compiler_params=pltpu.CompilerParams(
                collective_id=0, has_side_effects=True, vmem_limit_bytes=48 * 1024 * 1024
            ),
        )(
            tokens,
            gain,
            base_weight,
            down,
            up,
            row_adapter.reshape(1, rows),
            adapter_slot.reshape(1, -1),
        )

    return jax.shard_map(
        shards,
        mesh=mesh,
        in_specs=(
            P("parts", ("tensor", "rows")),
            P("section", None),
            P("section", None, ("tensor", "rows")),
            P("section", "tensor", None, "rows"),
            P("section", "tensor", None, "rows"),
            P("parts"),
            P(),
        ),
        out_specs=P(("parts", "section"), ("tensor", "rows")),
        check_vma=False,
    )
```

```python
import functools

import jax
import jax.numpy as jnp
from jax import lax
from jax.experimental import pallas as pl
from jax.experimental.pallas import tpu as pltpu
from jax.sharding import PartitionSpec as P

MESH = pl.DeviceIdType.MESH
epsilon = 1e-05


def crossed(position, offset, count):
    result = position
    bit = 1
    while bit < count:
        if offset & bit:
            result = result + bit - 2 * bit * lax.rem(lax.div(position, bit), 2)
        bit *= 2
    return result


def kernel(
    sections,
    tensors,
    tokens_ref,
    gain_ref,
    weight_ref,
    down_ref,
    up_ref,
    row_ref,
    slot_ref,
    out_ref,
    x_buf,
    w_buf,
    gain_buf,
    down_buf,
    up_buf,
    acc,
    normed,
    low_buf,
    chain_buf,
    out_buf,
    row_buf,
    slot_buf,
    token_sem,
    row_sem,
    slot_sem,
    gain_sem,
    down_sem,
    w_sem,
    x_send,
    x_recv,
    fwd_send,
    fwd_recv,
    up_send,
    up_recv,
    up_local,
    down_send,
    down_recv,
    low_send,
    low_recv,
    chain_send,
    out_send,
    out_recv,
    out_local,
):
    s = lax.axis_index("section")
    t = lax.axis_index("tensor")
    h = lax.axis_index("rows")
    other = 1 - h
    chunks, rows, piece = x_buf.shape[0], x_buf.shape[3], x_buf.shape[4]
    width = chunks * piece
    own_chunks = chunks // 2 if sections > 1 else chunks
    me = t * 2 + h
    peers = [crossed(t, j, tensors) for j in range(tensors)]
    pairs = [(j, hh) for j in range(tensors) for hh in range(2)]
    last = sections - 1

    def block_of(j, hh):
        return peers[j] * 2 + (h if hh == 0 else other)

    def token_copy(c):
        return pltpu.make_async_copy(
            tokens_ref.at[:, pl.ds(c * piece, piece)], x_buf.at[c, 0, 0], token_sem.at[c]
        )

    @pl.when(s == 0)
    def _():
        for c in range(chunks):
            token_copy(c).start()

    row_copy = pltpu.make_async_copy(row_ref, row_buf, row_sem)
    row_copy.start()
    slot_copy = pltpu.make_async_copy(slot_ref, slot_buf, slot_sem)
    slot_copy.start()
    gain_copy = pltpu.make_async_copy(gain_ref, gain_buf, gain_sem)
    gain_copy.start()
    down_copy = pltpu.make_async_copy(down_ref.at[0, 0], down_buf.at[h], down_sem)
    down_copy.start()

    def w_copy(c, j, hh):
        first = pl.multiple_of(block_of(j, hh) * width + c * piece, piece)
        return pltpu.make_async_copy(
            weight_ref.at[0, pl.ds(first, piece), :],
            w_buf.at[c, pl.ds((2 * j + hh) * piece, piece), :],
            w_sem.at[c, 2 * j + hh],
        )

    for c in range(chunks):
        for j, hh in pairs:
            w_copy(c, j, hh).start()

    barrier = pltpu.get_barrier_semaphore()

    def greet(device):
        pl.semaphore_signal(barrier, inc=1, device_id=device, device_id_type=MESH)

    for j, hh in pairs:
        if j or hh:
            greet({"tensor": peers[j], "rows": h if hh == 0 else other})
    expected = 2 * tensors - 1
    if sections > 1:

        @pl.when(s > 0)
        def _():
            for j in range(tensors):
                greet({"section": s - 1, "tensor": peers[j]})

        @pl.when(s < last)
        def _():
            for j in range(tensors):
                greet({"section": s + 1, "tensor": peers[j]})

        expected = expected + tensors * (
            jnp.where(s > 0, 1, 0) + jnp.where(s < last, 1, 0)
        )
    if sections > 2:

        @pl.when(s == last)
        def _():
            for d in range(last - 1):
                greet({"section": d})

        @pl.when(s < last - 1)
        def _():
            greet({"section": last})

        expected = (
            expected + jnp.where(s == last, last - 1, 0) + jnp.where(s < last - 1, 1, 0)
        )
    pl.semaphore_wait(barrier, expected)

    def token_send(c, j):
        return pltpu.make_async_remote_copy(
            src_ref=tokens_ref.at[:, pl.ds(c * piece, piece)],
            dst_ref=x_buf.at[c, j, 0],
            send_sem=x_send.at[c, j],
            recv_sem=x_recv.at[c, j],
            device_id={"section": 0, "tensor": peers[j]},
            device_id_type=MESH,
        )

    def chain(c, j):
        return pltpu.make_async_remote_copy(
            src_ref=chain_buf.at[c],
            dst_ref=x_buf.at[c, j, 0],
            send_sem=chain_send.at[c, j],
            recv_sem=x_recv.at[c, j],
            device_id={"section": lax.rem(s + 1, sections), "tensor": peers[j]},
            device_id_type=MESH,
        )

    def fwd_copy(c, j):
        return pltpu.make_async_remote_copy(
            src_ref=x_buf.at[c, j, 0],
            dst_ref=x_buf.at[c, j, 1],
            send_sem=fwd_send.at[c, j],
            recv_sem=fwd_recv.at[c, j],
            device_id={"rows": other},
            device_id_type=MESH,
        )

    @pl.when(s == 0)
    def _():
        for c in range(own_chunks):
            for j in range(1, tensors):
                token_send(c, j).start()

    if sections > 1:

        @pl.when(s == 1)
        def _():
            for c in range(own_chunks, chunks):
                for j in range(1, tensors):
                    token_send(c, j).start()

    down_remote = pltpu.make_async_remote_copy(
        src_ref=down_ref.at[0, 0],
        dst_ref=down_buf.at[h],
        send_sem=down_send,
        recv_sem=down_recv,
        device_id={"rows": other},
        device_id_type=MESH,
    )
    down_remote.start()

    def up_remote(i):
        dest = h * tensors + i
        return pltpu.make_async_remote_copy(
            src_ref=up_ref.at[0, 0, :, pl.ds(i * width, width)],
            dst_ref=up_buf.at[t],
            send_sem=up_send.at[i],
            recv_sem=up_recv.at[t],
            device_id={"tensor": lax.div(dest, 2), "rows": lax.rem(dest, 2)},
            device_id_type=MESH,
        )

    def up_here(i):
        return pltpu.make_async_copy(
            up_ref.at[0, 0, :, pl.ds(i * width, width)], up_buf.at[t], up_local
        )

    for i in range(tensors):

        @pl.when(h * tensors + i != me)
        def _():
            up_remote(i).start()

        @pl.when(h * tensors + i == me)
        def _():
            up_here(i).start()

    row_copy.wait()
    slot_copy.wait()
    row = row_buf[...]
    slots = slot_buf[...]
    slot_row = jnp.zeros_like(row)
    for a in range(slots.shape[1]):
        slot_row = jnp.where(row == a, slots[:, a : a + 1], slot_row)
    grid_shape = (rows, rows)
    diagonal = lax.broadcasted_iota(jnp.int32, grid_shape, 0) == lax.broadcasted_iota(
        jnp.int32, grid_shape, 1
    )
    spread = jnp.broadcast_to(slot_row.astype(jnp.float32), grid_shape)
    slot_column = jnp.sum(jnp.where(diagonal, spread, 0.0), axis=1, keepdims=True)
    hot_here = (slot_column == t.astype(jnp.float32)).astype(jnp.float32)

    gain_copy.wait()
    down_copy.wait()
    down_remote.wait_recv()
    squares = jnp.zeros((rows, piece), jnp.float32)
    score = jnp.zeros((rows, down_buf.shape[1]), jnp.float32)

    def low_copy(j):
        return pltpu.make_async_remote_copy(
            src_ref=low_buf.at[0],
            dst_ref=low_buf.at[j],
            send_sem=low_send.at[j],
            recv_sem=low_recv.at[j],
            device_id={"tensor": peers[j]},
            device_id_type=MESH,
        )

    for c in range(chunks):

        @pl.when(s == 0)
        def _():
            token_copy(c).wait()

        @pl.when(s > 0)
        def _():
            x_recv_own = chain(c, 0)
            x_recv_own.wait_recv()

        fwd_copy(c, 0).start()
        for j in range(1, tensors):
            chain(c, j).wait_recv()
            fwd_copy(c, j).start()
        for hh in range(2):
            for j in range(tensors):
                if hh == 1:
                    fwd_copy(c, j).wait_recv()
                values = x_buf[c, j, hh].astype(jnp.float32)
                squares = squares + values * values
                place = pl.multiple_of(block_of(j, hh) * width + c * piece, piece)
                normed[:, (2 * j + hh) * piece : (2 * j + hh + 1) * piece] = (
                    values * gain_buf[:, pl.ds(place, piece)]
                ).astype(jnp.bfloat16)
        downs = []
        for j, hh in pairs:
            block = block_of(j, hh)
            place = pl.multiple_of(lax.rem(block, tensors) * width + c * piece, piece)
            downs.append(down_buf[lax.div(block, tensors), :, pl.ds(place, piece)])
        score = score + lax.dot_general(
            normed[...],
            jnp.concatenate(downs, axis=1),
            (((1,), (1,)), ((), ())),
            preferred_element_type=jnp.float32,
        )
        if c == chunks - 1:
            mean_square = jnp.sum(squares, axis=1, keepdims=True) / (2 * tensors * width)
            scale = lax.rsqrt(mean_square + epsilon)
            low_buf[0] = (hot_here * score * scale).astype(jnp.bfloat16)
            for j in range(1, tensors):
                low_copy(j).start()
        for j, hh in pairs:
            w_copy(c, j, hh).wait()
        part = jnp.dot(normed[...], w_buf[c], preferred_element_type=jnp.float32)
        acc[...] = part if c == 0 else acc[...] + part

    half_here = lax.div(me, tensors)
    for k in range(tensors):
        local = (t == k) & (h == half_here)

        @pl.when(local)
        def _():
            up_here(0).wait()

        @pl.when(jnp.logical_not(local))
        def _():
            pltpu.make_async_remote_copy(
                src_ref=up_buf.at[k],
                dst_ref=up_buf.at[k],
                send_sem=up_send.at[0],
                recv_sem=up_recv.at[k],
                device_id={"rows": other},
                device_id_type=MESH,
            ).wait_recv()

    for j in range(1, tensors):
        low_copy(j).wait_recv()

    share = rows // sections
    for c in range(chunks):
        columns = slice(c * piece, (c + 1) * piece)
        update = jnp.zeros((rows, piece), jnp.float32)
        for j in range(tensors):
            update = update + jnp.dot(
                low_buf[j], up_buf[peers[j], :, columns], preferred_element_type=jnp.float32
            )
        total = x_buf[c, 0, 0].astype(jnp.float32) + scale * acc[:, columns] + 0.5 * update

        @pl.when(s < last)
        def _():
            chain_buf[c] = total.astype(jnp.bfloat16)
            for j in range(tensors):
                chain(c, j).start()

        @pl.when(s == last)
        def _():
            for d in range(sections):
                out_buf[d, :, columns] = total[d * share : (d + 1) * share].astype(jnp.bfloat16)

    def out_copy(d):
        return pltpu.make_async_remote_copy(
            src_ref=out_buf.at[d],
            dst_ref=out_ref,
            send_sem=out_send.at[d],
            recv_sem=out_recv,
            device_id={"section": d},
            device_id_type=MESH,
        )

    @pl.when(s == last)
    def _():
        for d in range(last):
            out_copy(d).start()
        here = pltpu.make_async_copy(out_buf.at[last], out_ref, out_local)
        here.start()
        here.wait()
        for d in range(last):
            out_copy(d).wait_send()

    @pl.when(s == 0)
    def _():
        for c in range(own_chunks):
            for j in range(1, tensors):
                token_send(c, j).wait_send()

    if sections > 1:

        @pl.when(s == 1)
        def _():
            for c in range(own_chunks, chunks):
                for j in range(1, tensors):
                    token_send(c, j).wait_send()

    for c in range(chunks):
        for j in range(tensors):
            fwd_copy(c, j).wait_send()
    for j in range(1, tensors):
        low_copy(j).wait_send()
    down_remote.wait_send()
    for i in range(tensors):

        @pl.when(h * tensors + i != me)
        def _():
            up_remote(i).wait_send()

    @pl.when(s < last)
    def _():
        for c in range(chunks):
            for j in range(tensors):
                chain(c, j).wait_send()
        out_copy(0).wait_recv()


def solution(mesh):
    sections, tensors = mesh.shape["section"], mesh.shape["tensor"]

    def shards(tokens, gain, base_weight, down, up, row_adapter, adapter_slot):
        rows, width = tokens.shape
        features = gain.shape[1]
        rank = down.shape[2]
        piece = max(128, width // 4)
        chunks = width // piece
        bf16, f32 = jnp.bfloat16, jnp.float32
        dma = pltpu.SemaphoreType.DMA
        hbm = pl.BlockSpec(memory_space=pltpu.HBM)
        return pl.pallas_call(
            functools.partial(kernel, sections, tensors),
            out_shape=jax.ShapeDtypeStruct((rows // sections, width), bf16),
            in_specs=[hbm] * 7,
            out_specs=hbm,
            scratch_shapes=[
                pltpu.VMEM((chunks, tensors, 2, rows, piece), bf16),
                pltpu.VMEM((chunks, 2 * tensors * piece, width), bf16),
                pltpu.VMEM((1, features), f32),
                pltpu.VMEM((2, rank, down.shape[3]), bf16),
                pltpu.VMEM((tensors, rank, width), bf16),
                pltpu.VMEM((rows, width), f32),
                pltpu.VMEM((rows, 2 * tensors * piece), bf16),
                pltpu.VMEM((tensors, rows, rank), bf16),
                pltpu.VMEM((chunks, rows, piece), bf16),
                pltpu.VMEM((sections, rows // sections, width), bf16),
                pltpu.VMEM((1, rows), jnp.int32),
                pltpu.VMEM((1, adapter_slot.shape[0]), jnp.int32),
                dma((chunks,)),
                dma,
                dma,
                dma,
                dma,
                dma((chunks, 2 * tensors)),
                dma((chunks, tensors)),
                dma((chunks, tensors)),
                dma((chunks, tensors)),
                dma((chunks, tensors)),
                dma((tensors,)),
                dma((tensors,)),
                dma,
                dma,
                dma,
                dma((tensors,)),
                dma((tensors,)),
                dma((chunks, tensors)),
                dma((sections,)),
                dma,
                dma,
            ],
            compiler_params=pltpu.CompilerParams(
                collective_id=0, has_side_effects=True, vmem_limit_bytes=64 * 1024 * 1024
            ),
        )(
            tokens,
            gain,
            base_weight,
            down,
            up,
            row_adapter.reshape(1, rows),
            adapter_slot.reshape(1, -1),
        )

    return jax.shard_map(
        shards,
        mesh=mesh,
        in_specs=(
            P("parts", ("tensor", "rows")),
            P("section", None),
            P("section", None, ("tensor", "rows")),
            P("section", "tensor", None, "rows"),
            P("section", "tensor", None, "rows"),
            P("parts"),
            P(),
        ),
        out_specs=P(("parts", "section"), ("tensor", "rows")),
        check_vma=False,
    )
```

```python
import functools

import jax
import jax.numpy as jnp
from jax import lax
from jax.experimental import pallas as pl
from jax.experimental.pallas import tpu as pltpu
from jax.sharding import PartitionSpec as P

MESH = pl.DeviceIdType.MESH
epsilon = 1e-05


def crossed(position, offset, count):
    result = position
    bit = 1
    while bit < count:
        if offset & bit:
            result = result + bit - 2 * bit * lax.rem(lax.div(position, bit), 2)
        bit *= 2
    return result


def kernel(
    sections,
    tensors,
    tokens_ref,
    gain_ref,
    weight_ref,
    down_ref,
    up_ref,
    row_ref,
    slot_ref,
    out_ref,
    x_buf,
    w_buf,
    gain_buf,
    down_buf,
    up_buf,
    acc,
    normed,
    squares,
    score,
    low_buf,
    low_all,
    part_down,
    part_score,
    chain_buf,
    out_buf,
    row_buf,
    slot_buf,
    token_sem,
    row_sem,
    slot_sem,
    gain_sem,
    down_sem,
    w_sem,
    x_send,
    x_recv,
    fwd_send,
    fwd_recv,
    up_send,
    up_recv,
    up_local,
    part_down_send,
    part_down_recv,
    part_down_local,
    part_send,
    part_recv,
    down_send,
    down_recv,
    low_send,
    low_recv,
    chain_send,
    out_send,
    out_recv,
    out_local,
):
    s = lax.axis_index("section")
    t = lax.axis_index("tensor")
    h = lax.axis_index("rows")
    other = 1 - h
    chunks, rows, piece = x_buf.shape[0], x_buf.shape[3], x_buf.shape[4]
    width = chunks * piece
    own_chunks = chunks // 2 if sections > 1 else chunks
    me = t * 2 + h
    peers = [crossed(t, j, tensors) for j in range(tensors)]
    pairs = [(j, hh) for j in range(tensors) for hh in range(2)]
    last = sections - 1
    order = sorted(range(chunks), key=lambda c: (c % max(1, chunks // 2), c))

    def block_of(j, hh):
        return peers[j] * 2 + (h if hh == 0 else other)

    barrier = pltpu.get_barrier_semaphore()

    def greet(device):
        pl.semaphore_signal(barrier, inc=1, device_id=device, device_id_type=MESH)

    for j, hh in pairs:
        if j or hh:
            greet({"tensor": peers[j], "rows": h if hh == 0 else other})
    expected = 2 * tensors - 1
    if sections > 1:

        @pl.when(s > 0)
        def _():
            for j in range(tensors):
                greet({"section": s - 1, "tensor": peers[j]})

        @pl.when(s < last)
        def _():
            for j in range(tensors):
                greet({"section": s + 1, "tensor": peers[j]})

        expected = expected + tensors * (
            jnp.where(s > 0, 1, 0) + jnp.where(s < last, 1, 0)
        )
    if sections > 2:

        @pl.when(s == last)
        def _():
            for d in range(last - 1):
                greet({"section": d})

        @pl.when(s < last - 1)
        def _():
            greet({"section": last})

        expected = (
            expected + jnp.where(s == last, last - 1, 0) + jnp.where(s < last - 1, 1, 0)
        )
    def token_copy(c):
        return pltpu.make_async_copy(
            tokens_ref.at[:, pl.ds(c * piece, piece)], x_buf.at[c, 0, 0], token_sem.at[c]
        )

    @pl.when(s == 0)
    def _():
        for c in range(chunks):
            token_copy(c).start()

    row_copy = pltpu.make_async_copy(row_ref, row_buf, row_sem)
    row_copy.start()
    slot_copy = pltpu.make_async_copy(slot_ref, slot_buf, slot_sem)
    slot_copy.start()
    gain_copy = pltpu.make_async_copy(gain_ref, gain_buf, gain_sem)
    gain_copy.start()
    down_copy = pltpu.make_async_copy(down_ref.at[0, 0], down_buf.at[h], down_sem)

    @pl.when(s == 0)
    def _():
        down_copy.start()

    def w_copy(c, j, hh):
        first = pl.multiple_of(block_of(j, hh) * width + c * piece, piece)
        return pltpu.make_async_copy(
            weight_ref.at[0, pl.ds(first, piece), :],
            w_buf.at[c, pl.ds((2 * j + hh) * piece, piece), :],
            w_sem.at[c, 2 * j + hh],
        )

    for c in range(chunks):
        for j, hh in pairs:
            w_copy(c, j, hh).start()

    pl.semaphore_wait(barrier, expected)

    def token_send(c, j):
        return pltpu.make_async_remote_copy(
            src_ref=tokens_ref.at[:, pl.ds(c * piece, piece)],
            dst_ref=x_buf.at[c, j, 0],
            send_sem=x_send.at[c, j],
            recv_sem=x_recv.at[c, j],
            device_id={"section": 0, "tensor": peers[j]},
            device_id_type=MESH,
        )

    def chain(c, j):
        return pltpu.make_async_remote_copy(
            src_ref=chain_buf.at[c],
            dst_ref=x_buf.at[c, j, 0],
            send_sem=chain_send.at[c, j],
            recv_sem=x_recv.at[c, j],
            device_id={"section": lax.rem(s + 1, sections), "tensor": peers[j]},
            device_id_type=MESH,
        )

    def fwd_copy(c, j):
        return pltpu.make_async_remote_copy(
            src_ref=x_buf.at[c, j, 0],
            dst_ref=x_buf.at[c, j, 1],
            send_sem=fwd_send.at[c, j],
            recv_sem=fwd_recv.at[c, j],
            device_id={"rows": other},
            device_id_type=MESH,
        )

    @pl.when(s == 0)
    def _():
        for c in range(own_chunks):
            for j in range(1, tensors):
                token_send(c, j).start()

    if sections > 1:

        @pl.when(s == 1)
        def _():
            for c in range(own_chunks, chunks):
                for j in range(1, tensors):
                    token_send(c, j).start()

    down_remote = pltpu.make_async_remote_copy(
        src_ref=down_ref.at[0, 0],
        dst_ref=down_buf.at[h],
        send_sem=down_send,
        recv_sem=down_recv,
        device_id={"rows": other},
        device_id_type=MESH,
    )

    @pl.when(s == 0)
    def _():
        down_remote.start()

    def map_remote(i, source, landing, sent, landed):
        dest = h * tensors + i
        return pltpu.make_async_remote_copy(
            src_ref=source.at[0, 0, :, pl.ds(i * width, width)],
            dst_ref=landing.at[t],
            send_sem=sent.at[i],
            recv_sem=landed.at[t],
            device_id={"tensor": lax.div(dest, 2), "rows": lax.rem(dest, 2)},
            device_id_type=MESH,
        )

    def map_here(i, source, landing, done):
        return pltpu.make_async_copy(
            source.at[0, 0, :, pl.ds(i * width, width)], landing.at[t], done
        )

    def send_maps(source, landing, sent, landed, done):
        for i in range(tensors):

            @pl.when(h * tensors + i != me)
            def _():
                map_remote(i, source, landing, sent, landed).start()

            @pl.when(h * tensors + i == me)
            def _():
                map_here(i, source, landing, done).start()

    def wait_maps(source, landing, sent, landed, done):
        half_here = lax.div(me, tensors)
        for k in range(tensors):
            local = (t == k) & (h == half_here)

            @pl.when(local)
            def _():
                map_here(0, source, landing, done).wait()

            @pl.when(jnp.logical_not(local))
            def _():
                pltpu.make_async_remote_copy(
                    src_ref=landing.at[k],
                    dst_ref=landing.at[k],
                    send_sem=sent.at[0],
                    recv_sem=landed.at[k],
                    device_id={"rows": other},
                    device_id_type=MESH,
                ).wait_recv()

    def wait_maps_sent(source, landing, sent, landed, done):
        for i in range(tensors):

            @pl.when(h * tensors + i != me)
            def _():
                map_remote(i, source, landing, sent, landed).wait_send()

    ups = (up_ref, up_buf, up_send, up_recv, up_local)
    downs = (down_ref, part_down, part_down_send, part_down_recv, part_down_local)

    @pl.when(s > 0)
    def _():
        send_maps(*downs)

    send_maps(*ups)

    row_copy.wait()
    slot_copy.wait()
    row = row_buf[...]
    slots = slot_buf[...]
    slot_row = jnp.zeros_like(row)
    for a in range(slots.shape[1]):
        slot_row = jnp.where(row == a, slots[:, a : a + 1], slot_row)
    grid_shape = (rows, rows)
    diagonal = lax.broadcasted_iota(jnp.int32, grid_shape, 0) == lax.broadcasted_iota(
        jnp.int32, grid_shape, 1
    )
    spread = jnp.broadcast_to(slot_row.astype(jnp.float32), grid_shape)
    slot_column = jnp.sum(jnp.where(diagonal, spread, 0.0), axis=1, keepdims=True)
    hot_here = (slot_column == t.astype(jnp.float32)).astype(jnp.float32)
    rank = down_buf.shape[1]

    gain_copy.wait()

    def low_copy(j):
        return pltpu.make_async_remote_copy(
            src_ref=low_buf.at[0],
            dst_ref=low_buf.at[j],
            send_sem=low_send.at[j],
            recv_sem=low_recv.at[j],
            device_id={"tensor": peers[j]},
            device_id_type=MESH,
        )

    def part_copy(j, hh):
        return pltpu.make_async_remote_copy(
            src_ref=part_score.at[0],
            dst_ref=part_score.at[2 * j + hh],
            send_sem=part_send.at[2 * j + hh],
            recv_sem=part_recv.at[2 * j + hh],
            device_id={"tensor": peers[j], "rows": h if hh == 0 else other},
            device_id_type=MESH,
        )

    def absorb(c, j, hh):
        values = x_buf[c, j, hh].astype(jnp.float32)
        if c == 0 and j == 0 and hh == 0:
            squares[...] = values * values
        else:
            squares[...] += values * values
        place = pl.multiple_of(block_of(j, hh) * width + c * piece, piece)
        normed[c, :, (2 * j + hh) * piece : (2 * j + hh + 1) * piece] = (
            values * gain_buf[:, pl.ds(place, piece)]
        ).astype(jnp.bfloat16)

    def multiply(c):
        for j, hh in pairs:
            w_copy(c, j, hh).wait()
        part = jnp.dot(normed[c], w_buf[c], preferred_element_type=jnp.float32)
        acc[...] = part if c == order[0] else acc[...] + part

    for c in range(chunks):

        @pl.when(s == 0)
        def _():
            token_copy(c).wait()

        @pl.when(s > 0)
        def _():
            chain(c, 0).wait_recv()

        fwd_copy(c, 0).start()
        absorb(c, 0, 0)

    @pl.when(s > 0)
    def _():
        wait_maps(*downs)
        shape = (rows, tensors * rank)
        own = jnp.zeros(shape, jnp.float32)
        for c in range(chunks):
            own = own + lax.dot_general(
                normed[c, :, :piece],
                jnp.concatenate(
                    [part_down[k, :, c * piece : (c + 1) * piece] for k in range(tensors)], axis=0
                ),
                (((1,), (1,)), ((), ())),
                preferred_element_type=jnp.float32,
            )
        slot_of_lane = lax.div(lax.broadcasted_iota(jnp.int32, shape, 1), rank)
        kept = slot_of_lane.astype(jnp.float32) == slot_column
        part_score[0] = jnp.where(kept, own, 0.0).astype(jnp.bfloat16)
        for j, hh in pairs:
            if j or hh:
                part_copy(j, hh).start()

    @pl.when(s == 0)
    def _():
        down_copy.wait()
        down_remote.wait_recv()

    for step in range(chunks + 1):
        if step < chunks:
            for j in range(1, tensors):
                chain(order[step], j).wait_recv()
                fwd_copy(order[step], j).start()
        if step == 0:
            continue
        c = order[step - 1]
        for j in range(1, tensors):
            absorb(c, j, 0)
        for j in range(tensors):
            fwd_copy(c, j).wait_recv()
            absorb(c, j, 1)

        @pl.when(s == 0)
        def _():
            down_pieces = []
            for j, hh in pairs:
                block = block_of(j, hh)
                place = pl.multiple_of(lax.rem(block, tensors) * width + c * piece, piece)
                down_pieces.append(down_buf[lax.div(block, tensors), :, pl.ds(place, piece)])
            score_part = lax.dot_general(
                normed[c],
                jnp.concatenate(down_pieces, axis=1),
                (((1,), (1,)), ((), ())),
                preferred_element_type=jnp.float32,
            )
            score[...] = score_part if step == 1 else score[...] + score_part

        if step <= chunks - 2:
            multiply(c)

    mean_square = jnp.sum(squares[...], axis=1, keepdims=True) / (2 * tensors * width)
    scale = lax.rsqrt(mean_square + epsilon)

    @pl.when(s == 0)
    def _():
        low_buf[0] = (hot_here * score[...] * scale).astype(jnp.bfloat16)
        for j in range(1, tensors):
            low_copy(j).start()

    for c in order[max(chunks - 2, 0) :]:
        multiply(c)

    wait_maps(*ups)

    @pl.when(s == 0)
    def _():
        for j in range(1, tensors):
            low_copy(j).wait_recv()
        for k in range(tensors):
            low_all[:, k * rank : (k + 1) * rank] = low_buf[peers[k]]

    @pl.when(s > 0)
    def _():
        summed = part_score[0].astype(jnp.float32)
        for j, hh in pairs:
            if j or hh:
                part_copy(j, hh).wait_recv()
                summed = summed + part_score[2 * j + hh].astype(jnp.float32)
        low_all[...] = (summed * scale).astype(jnp.bfloat16)

    share = rows // sections

    def out_copy(c, d):
        return pltpu.make_async_remote_copy(
            src_ref=out_buf.at[c, d],
            dst_ref=out_ref.at[:, pl.ds(c * piece, piece)],
            send_sem=out_send.at[c, d],
            recv_sem=out_recv.at[c],
            device_id={"section": d},
            device_id_type=MESH,
        )

    def out_here(c):
        return pltpu.make_async_copy(
            out_buf.at[c, last], out_ref.at[:, pl.ds(c * piece, piece)], out_local.at[c]
        )

    for c in range(chunks):
        columns = slice(c * piece, (c + 1) * piece)
        update = jnp.dot(
            low_all[...],
            jnp.concatenate([up_buf[k, :, columns] for k in range(tensors)], axis=0),
            preferred_element_type=jnp.float32,
        )
        total = x_buf[c, 0, 0].astype(jnp.float32) + scale * acc[:, columns] + 0.5 * update

        @pl.when(s < last)
        def _():
            chain_buf[c] = total.astype(jnp.bfloat16)
            chain(c, 0).start()

        @pl.when(s == last)
        def _():
            for d in range(sections):
                out_buf[c, d] = total[d * share : (d + 1) * share].astype(jnp.bfloat16)
                if d < last:
                    out_copy(c, d).start()
                else:
                    out_here(c).start()

    @pl.when(s < last)
    def _():
        for c in order:
            for j in range(1, tensors):
                chain(c, j).start()

    @pl.when(s == last)
    def _():
        for c in range(chunks):
            out_here(c).wait()
            for d in range(last):
                out_copy(c, d).wait_send()

    @pl.when(s == 0)
    def _():
        for c in range(own_chunks):
            for j in range(1, tensors):
                token_send(c, j).wait_send()

    if sections > 1:

        @pl.when(s == 1)
        def _():
            for c in range(own_chunks, chunks):
                for j in range(1, tensors):
                    token_send(c, j).wait_send()

    for c in range(chunks):
        for j in range(tensors):
            fwd_copy(c, j).wait_send()
    wait_maps_sent(*ups)

    @pl.when(s == 0)
    def _():
        for j in range(1, tensors):
            low_copy(j).wait_send()
        down_remote.wait_send()

    @pl.when(s > 0)
    def _():
        wait_maps_sent(*downs)
        for j, hh in pairs:
            if j or hh:
                part_copy(j, hh).wait_send()

    @pl.when(s < last)
    def _():
        for c in range(chunks):
            for j in range(tensors):
                chain(c, j).wait_send()
        for c in range(chunks):
            out_copy(c, 0).wait_recv()


def solution(mesh):
    sections, tensors = mesh.shape["section"], mesh.shape["tensor"]

    def shards(tokens, gain, base_weight, down, up, row_adapter, adapter_slot):
        rows, width = tokens.shape
        features = gain.shape[1]
        rank = down.shape[2]
        piece = max(128, width // 4)
        chunks = width // piece
        bf16, f32 = jnp.bfloat16, jnp.float32
        dma = pltpu.SemaphoreType.DMA
        hbm = pl.BlockSpec(memory_space=pltpu.HBM)
        return pl.pallas_call(
            functools.partial(kernel, sections, tensors),
            out_shape=jax.ShapeDtypeStruct((rows // sections, width), bf16),
            in_specs=[hbm] * 7,
            out_specs=hbm,
            scratch_shapes=[
                pltpu.VMEM((chunks, tensors, 2, rows, piece), bf16),
                pltpu.VMEM((chunks, 2 * tensors * piece, width), bf16),
                pltpu.VMEM((1, features), f32),
                pltpu.VMEM((2, rank, down.shape[3]), bf16),
                pltpu.VMEM((tensors, rank, width), bf16),
                pltpu.VMEM((rows, width), f32),
                pltpu.VMEM((chunks, rows, 2 * tensors * piece), bf16),
                pltpu.VMEM((rows, piece), f32),
                pltpu.VMEM((rows, rank), f32),
                pltpu.VMEM((tensors, rows, rank), bf16),
                pltpu.VMEM((rows, tensors * rank), bf16),
                pltpu.VMEM((tensors, rank, width), bf16),
                pltpu.VMEM((2 * tensors, rows, tensors * rank), bf16),
                pltpu.VMEM((chunks, rows, piece), bf16),
                pltpu.VMEM((chunks, sections, rows // sections, piece), bf16),
                pltpu.VMEM((1, rows), jnp.int32),
                pltpu.VMEM((1, adapter_slot.shape[0]), jnp.int32),
                dma((chunks,)),
                dma,
                dma,
                dma,
                dma,
                dma((chunks, 2 * tensors)),
                dma((chunks, tensors)),
                dma((chunks, tensors)),
                dma((chunks, tensors)),
                dma((chunks, tensors)),
                dma((tensors,)),
                dma((tensors,)),
                dma,
                dma((tensors,)),
                dma((tensors,)),
                dma,
                dma((2 * tensors,)),
                dma((2 * tensors,)),
                dma,
                dma,
                dma((tensors,)),
                dma((tensors,)),
                dma((chunks, tensors)),
                dma((chunks, sections)),
                dma((chunks,)),
                dma((chunks,)),
            ],
            compiler_params=pltpu.CompilerParams(
                collective_id=0, has_side_effects=True, vmem_limit_bytes=64 * 1024 * 1024
            ),
        )(
            tokens,
            gain,
            base_weight,
            down,
            up,
            row_adapter.reshape(1, rows),
            adapter_slot.reshape(1, -1),
        )

    return jax.shard_map(
        shards,
        mesh=mesh,
        in_specs=(
            P("parts", ("tensor", "rows")),
            P("section", None),
            P("section", None, ("tensor", "rows")),
            P("section", "tensor", None, "rows"),
            P("section", "tensor", None, "rows"),
            P("parts"),
            P(),
        ),
        out_specs=P(("parts", "section"), ("tensor", "rows")),
        check_vma=False,
    )
```

```python
import functools

import jax
import jax.numpy as jnp
from jax import lax
from jax.experimental import pallas as pl
from jax.experimental.pallas import tpu as pltpu
from jax.sharding import PartitionSpec as P

MESH = pl.DeviceIdType.MESH
epsilon = 1e-05


def crossed(position, offset, count):
    result = position
    bit = 1
    while bit < count:
        if offset & bit:
            result = result + bit - 2 * bit * lax.rem(lax.div(position, bit), 2)
        bit *= 2
    return result


def kernel(
    sections,
    tensors,
    tokens_ref,
    gain_ref,
    weight_ref,
    down_ref,
    up_ref,
    row_ref,
    slot_ref,
    out_ref,
    x_buf,
    w_buf,
    gain_buf,
    down_buf,
    up_buf,
    acc,
    normed,
    squares,
    score,
    low_buf,
    low_all,
    part_down,
    part_score,
    chain_buf,
    out_buf,
    row_buf,
    slot_buf,
    token_sem,
    row_sem,
    slot_sem,
    gain_sem,
    down_sem,
    w_sem,
    x_send,
    x_recv,
    fwd_send,
    fwd_recv,
    up_send,
    up_recv,
    up_local,
    part_down_send,
    part_down_recv,
    part_down_local,
    part_send,
    part_recv,
    down_send,
    down_recv,
    low_send,
    low_recv,
    chain_send,
    out_send,
    out_recv,
    out_local,
):
    s = lax.axis_index("section")
    t = lax.axis_index("tensor")
    h = lax.axis_index("rows")
    other = 1 - h
    chunks, rows, piece = x_buf.shape[0], x_buf.shape[3], x_buf.shape[4]
    width = chunks * piece
    own_chunks = chunks // 2 if sections > 1 else chunks
    me = t * 2 + h
    peers = [crossed(t, j, tensors) for j in range(tensors)]
    pairs = [(j, hh) for j in range(tensors) for hh in range(2)]
    last = sections - 1
    order = sorted(range(chunks), key=lambda c: (c % max(1, chunks // 2), -c))

    def block_of(j, hh):
        return peers[j] * 2 + (h if hh == 0 else other)

    barrier = pltpu.get_barrier_semaphore()

    def greet(device):
        pl.semaphore_signal(barrier, inc=1, device_id=device, device_id_type=MESH)

    for j, hh in pairs:
        if j or hh:
            greet({"tensor": peers[j], "rows": h if hh == 0 else other})
    expected = 2 * tensors - 1
    if sections > 1:

        @pl.when(s > 0)
        def _():
            for j in range(tensors):
                greet({"section": s - 1, "tensor": peers[j]})

        @pl.when(s < last)
        def _():
            for j in range(tensors):
                greet({"section": s + 1, "tensor": peers[j]})

        expected = expected + tensors * (
            jnp.where(s > 0, 1, 0) + jnp.where(s < last, 1, 0)
        )
    if sections > 2:

        @pl.when(s == last)
        def _():
            for d in range(last - 1):
                greet({"section": d})

        @pl.when(s < last - 1)
        def _():
            greet({"section": last})

        expected = (
            expected + jnp.where(s == last, last - 1, 0) + jnp.where(s < last - 1, 1, 0)
        )
    def token_copy(c):
        return pltpu.make_async_copy(
            tokens_ref.at[:, pl.ds(c * piece, piece)], x_buf.at[c, 0, 0], token_sem.at[c]
        )

    @pl.when(s == 0)
    def _():
        for c in range(chunks):
            token_copy(c).start()

    row_copy = pltpu.make_async_copy(row_ref, row_buf, row_sem)
    row_copy.start()
    slot_copy = pltpu.make_async_copy(slot_ref, slot_buf, slot_sem)
    slot_copy.start()
    gain_copy = pltpu.make_async_copy(gain_ref, gain_buf, gain_sem)
    gain_copy.start()
    down_copy = pltpu.make_async_copy(down_ref.at[0, 0], down_buf.at[h], down_sem)

    @pl.when(s == 0)
    def _():
        down_copy.start()

    def w_copy(c, j, hh):
        first = pl.multiple_of(block_of(j, hh) * width + c * piece, piece)
        return pltpu.make_async_copy(
            weight_ref.at[0, pl.ds(first, piece), :],
            w_buf.at[c, pl.ds((2 * j + hh) * piece, piece), :],
            w_sem.at[c, 2 * j + hh],
        )

    for c in range(chunks):
        for j, hh in pairs:
            w_copy(c, j, hh).start()

    pl.semaphore_wait(barrier, expected)

    def token_send(c, j):
        return pltpu.make_async_remote_copy(
            src_ref=tokens_ref.at[:, pl.ds(c * piece, piece)],
            dst_ref=x_buf.at[c, j, 0],
            send_sem=x_send.at[c, j],
            recv_sem=x_recv.at[c, j],
            device_id={"section": 0, "tensor": peers[j]},
            device_id_type=MESH,
        )

    def chain(c, j):
        return pltpu.make_async_remote_copy(
            src_ref=chain_buf.at[c],
            dst_ref=x_buf.at[c, j, 0],
            send_sem=chain_send.at[c, j],
            recv_sem=x_recv.at[c, j],
            device_id={"section": lax.rem(s + 1, sections), "tensor": peers[j]},
            device_id_type=MESH,
        )

    def spread_copy(j):
        return pltpu.make_async_remote_copy(
            src_ref=x_buf.at[0, 0, 0],
            dst_ref=x_buf.at[0, j, 0],
            send_sem=x_send.at[0, j],
            recv_sem=x_recv.at[0, j],
            device_id={"tensor": peers[j]},
            device_id_type=MESH,
        )

    def fwd_copy(c, j):
        return pltpu.make_async_remote_copy(
            src_ref=x_buf.at[c, j, 0],
            dst_ref=x_buf.at[c, j, 1],
            send_sem=fwd_send.at[c, j],
            recv_sem=fwd_recv.at[c, j],
            device_id={"rows": other},
            device_id_type=MESH,
        )

    @pl.when(s == 0)
    def _():
        for c in range(own_chunks):
            for j in range(1, tensors):
                token_send(c, j).start()

    if sections > 1:

        @pl.when(s == 1)
        def _():
            for c in range(own_chunks, chunks):
                for j in range(1, tensors):
                    token_send(c, j).start()

    down_remote = pltpu.make_async_remote_copy(
        src_ref=down_ref.at[0, 0],
        dst_ref=down_buf.at[h],
        send_sem=down_send,
        recv_sem=down_recv,
        device_id={"rows": other},
        device_id_type=MESH,
    )

    @pl.when(s == 0)
    def _():
        down_remote.start()

    def map_remote(i, source, landing, sent, landed):
        dest = h * tensors + i
        return pltpu.make_async_remote_copy(
            src_ref=source.at[0, 0, :, pl.ds(i * width, width)],
            dst_ref=landing.at[t],
            send_sem=sent.at[i],
            recv_sem=landed.at[t],
            device_id={"tensor": lax.div(dest, 2), "rows": lax.rem(dest, 2)},
            device_id_type=MESH,
        )

    def map_here(i, source, landing, done):
        return pltpu.make_async_copy(
            source.at[0, 0, :, pl.ds(i * width, width)], landing.at[t], done
        )

    def send_maps(source, landing, sent, landed, done):
        for i in range(tensors):

            @pl.when(h * tensors + i != me)
            def _():
                map_remote(i, source, landing, sent, landed).start()

            @pl.when(h * tensors + i == me)
            def _():
                map_here(i, source, landing, done).start()

    def wait_maps(source, landing, sent, landed, done):
        half_here = lax.div(me, tensors)
        for k in range(tensors):
            local = (t == k) & (h == half_here)

            @pl.when(local)
            def _():
                map_here(0, source, landing, done).wait()

            @pl.when(jnp.logical_not(local))
            def _():
                pltpu.make_async_remote_copy(
                    src_ref=landing.at[k],
                    dst_ref=landing.at[k],
                    send_sem=sent.at[0],
                    recv_sem=landed.at[k],
                    device_id={"rows": other},
                    device_id_type=MESH,
                ).wait_recv()

    def wait_maps_sent(source, landing, sent, landed, done):
        for i in range(tensors):

            @pl.when(h * tensors + i != me)
            def _():
                map_remote(i, source, landing, sent, landed).wait_send()

    ups = (up_ref, up_buf, up_send, up_recv, up_local)
    downs = (down_ref, part_down, part_down_send, part_down_recv, part_down_local)

    @pl.when(s > 0)
    def _():
        send_maps(*downs)

    send_maps(*ups)

    row_copy.wait()
    slot_copy.wait()
    row = row_buf[...]
    slots = slot_buf[...]
    slot_row = jnp.zeros_like(row)
    for a in range(slots.shape[1]):
        slot_row = jnp.where(row == a, slots[:, a : a + 1], slot_row)
    grid_shape = (rows, rows)
    diagonal = lax.broadcasted_iota(jnp.int32, grid_shape, 0) == lax.broadcasted_iota(
        jnp.int32, grid_shape, 1
    )
    spread = jnp.broadcast_to(slot_row.astype(jnp.float32), grid_shape)
    slot_column = jnp.sum(jnp.where(diagonal, spread, 0.0), axis=1, keepdims=True)
    hot_here = (slot_column == t.astype(jnp.float32)).astype(jnp.float32)
    rank = down_buf.shape[1]

    gain_copy.wait()

    def low_copy(j):
        return pltpu.make_async_remote_copy(
            src_ref=low_buf.at[0],
            dst_ref=low_buf.at[j],
            send_sem=low_send.at[j],
            recv_sem=low_recv.at[j],
            device_id={"tensor": peers[j]},
            device_id_type=MESH,
        )

    def part_copy(j, hh):
        return pltpu.make_async_remote_copy(
            src_ref=part_score.at[0],
            dst_ref=part_score.at[2 * j + hh],
            send_sem=part_send.at[2 * j + hh],
            recv_sem=part_recv.at[2 * j + hh],
            device_id={"tensor": peers[j], "rows": h if hh == 0 else other},
            device_id_type=MESH,
        )

    def absorb(c, j, hh):
        values = x_buf[c, j, hh].astype(jnp.float32)
        if c == 0 and j == 0 and hh == 0:
            squares[...] = values * values
        else:
            squares[...] += values * values
        place = pl.multiple_of(block_of(j, hh) * width + c * piece, piece)
        normed[c, :, (2 * j + hh) * piece : (2 * j + hh + 1) * piece] = (
            values * gain_buf[:, pl.ds(place, piece)]
        ).astype(jnp.bfloat16)

    def multiply(c):
        for j, hh in pairs:
            w_copy(c, j, hh).wait()
        part = jnp.dot(normed[c], w_buf[c], preferred_element_type=jnp.float32)
        acc[...] = part if c == order[0] else acc[...] + part

    for c in range(chunks):

        @pl.when(s == 0)
        def _():
            token_copy(c).wait()

        @pl.when(s > 0)
        def _():
            chain(c, 0).wait_recv()
            if c == 0:
                for j in range(1, tensors):
                    spread_copy(j).start()

        fwd_copy(c, 0).start()
        absorb(c, 0, 0)

    @pl.when(s > 0)
    def _():
        wait_maps(*downs)
        shape = (rows, tensors * rank)
        own = jnp.zeros(shape, jnp.float32)
        for c in range(chunks):
            own = own + lax.dot_general(
                normed[c, :, :piece],
                jnp.concatenate(
                    [part_down[k, :, c * piece : (c + 1) * piece] for k in range(tensors)], axis=0
                ),
                (((1,), (1,)), ((), ())),
                preferred_element_type=jnp.float32,
            )
        slot_of_lane = lax.div(lax.broadcasted_iota(jnp.int32, shape, 1), rank)
        kept = slot_of_lane.astype(jnp.float32) == slot_column
        part_score[0] = jnp.where(kept, own, 0.0).astype(jnp.bfloat16)
        for j, hh in pairs:
            if j or hh:
                part_copy(j, hh).start()

    @pl.when(s == 0)
    def _():
        down_copy.wait()
        down_remote.wait_recv()

    for step in range(chunks + 1):
        if step < chunks:
            for j in range(1, tensors):
                chain(order[step], j).wait_recv()
                fwd_copy(order[step], j).start()
        if step == 0:
            continue
        c = order[step - 1]
        for j in range(1, tensors):
            absorb(c, j, 0)
        for j in range(tensors):
            fwd_copy(c, j).wait_recv()
            absorb(c, j, 1)

        @pl.when(s == 0)
        def _():
            down_pieces = []
            for j, hh in pairs:
                block = block_of(j, hh)
                place = pl.multiple_of(lax.rem(block, tensors) * width + c * piece, piece)
                down_pieces.append(down_buf[lax.div(block, tensors), :, pl.ds(place, piece)])
            score_part = lax.dot_general(
                normed[c],
                jnp.concatenate(down_pieces, axis=1),
                (((1,), (1,)), ((), ())),
                preferred_element_type=jnp.float32,
            )
            score[...] = score_part if step == 1 else score[...] + score_part

        if step <= chunks - 1:
            multiply(c)

    mean_square = jnp.sum(squares[...], axis=1, keepdims=True) / (2 * tensors * width)
    scale = lax.rsqrt(mean_square + epsilon)

    @pl.when(s == 0)
    def _():
        low_buf[0] = (hot_here * score[...] * scale).astype(jnp.bfloat16)
        for j in range(1, tensors):
            low_copy(j).start()

    multiply(order[-1])

    wait_maps(*ups)

    @pl.when(s == 0)
    def _():
        for j in range(1, tensors):
            low_copy(j).wait_recv()
        for k in range(tensors):
            low_all[:, k * rank : (k + 1) * rank] = low_buf[peers[k]]

    @pl.when(s > 0)
    def _():
        summed = part_score[0].astype(jnp.float32)
        for j, hh in pairs:
            if j or hh:
                part_copy(j, hh).wait_recv()
                summed = summed + part_score[2 * j + hh].astype(jnp.float32)
        low_all[...] = (summed * scale).astype(jnp.bfloat16)

    share = rows // sections

    def out_copy(c, d):
        return pltpu.make_async_remote_copy(
            src_ref=out_buf.at[c, d],
            dst_ref=out_ref.at[:, pl.ds(c * piece, piece)],
            send_sem=out_send.at[c, d],
            recv_sem=out_recv.at[c],
            device_id={"section": d},
            device_id_type=MESH,
        )

    def out_here(c):
        return pltpu.make_async_copy(
            out_buf.at[c, last], out_ref.at[:, pl.ds(c * piece, piece)], out_local.at[c]
        )

    for c in range(chunks):
        columns = slice(c * piece, (c + 1) * piece)
        update = jnp.dot(
            low_all[...],
            jnp.concatenate([up_buf[k, :, columns] for k in range(tensors)], axis=0),
            preferred_element_type=jnp.float32,
        )
        total = x_buf[c, 0, 0].astype(jnp.float32) + scale * acc[:, columns] + 0.5 * update

        @pl.when(s < last)
        def _():
            chain_buf[c] = total.astype(jnp.bfloat16)
            chain(c, 0).start()

        @pl.when(s == last)
        def _():
            for d in range(sections):
                out_buf[c, d] = total[d * share : (d + 1) * share].astype(jnp.bfloat16)
                if d < last:
                    out_copy(c, d).start()
                else:
                    out_here(c).start()

    @pl.when(s < last)
    def _():
        for c in order:
            if c > 0:
                for j in range(1, tensors):
                    chain(c, j).start()

    @pl.when(s == last)
    def _():
        for c in range(chunks):
            out_here(c).wait()
            for d in range(last):
                out_copy(c, d).wait_send()

    @pl.when(s == 0)
    def _():
        for c in range(own_chunks):
            for j in range(1, tensors):
                token_send(c, j).wait_send()

    if sections > 1:

        @pl.when(s == 1)
        def _():
            for c in range(own_chunks, chunks):
                for j in range(1, tensors):
                    token_send(c, j).wait_send()

    for c in range(chunks):
        for j in range(tensors):
            fwd_copy(c, j).wait_send()
    wait_maps_sent(*ups)

    @pl.when(s == 0)
    def _():
        for j in range(1, tensors):
            low_copy(j).wait_send()
        down_remote.wait_send()

    @pl.when(s > 0)
    def _():
        for j in range(1, tensors):
            spread_copy(j).wait_send()
        wait_maps_sent(*downs)
        for j, hh in pairs:
            if j or hh:
                part_copy(j, hh).wait_send()

    @pl.when(s < last)
    def _():
        for c in range(chunks):
            for j in range(tensors if c > 0 else 1):
                chain(c, j).wait_send()
        for c in range(chunks):
            out_copy(c, 0).wait_recv()


def solution(mesh):
    sections, tensors = mesh.shape["section"], mesh.shape["tensor"]

    def shards(tokens, gain, base_weight, down, up, row_adapter, adapter_slot):
        rows, width = tokens.shape
        features = gain.shape[1]
        rank = down.shape[2]
        piece = max(128, width // 4)
        chunks = width // piece
        bf16, f32 = jnp.bfloat16, jnp.float32
        dma = pltpu.SemaphoreType.DMA
        hbm = pl.BlockSpec(memory_space=pltpu.HBM)
        return pl.pallas_call(
            functools.partial(kernel, sections, tensors),
            out_shape=jax.ShapeDtypeStruct((rows // sections, width), bf16),
            in_specs=[hbm] * 7,
            out_specs=hbm,
            scratch_shapes=[
                pltpu.VMEM((chunks, tensors, 2, rows, piece), bf16),
                pltpu.VMEM((chunks, 2 * tensors * piece, width), bf16),
                pltpu.VMEM((1, features), f32),
                pltpu.VMEM((2, rank, down.shape[3]), bf16),
                pltpu.VMEM((tensors, rank, width), bf16),
                pltpu.VMEM((rows, width), f32),
                pltpu.VMEM((chunks, rows, 2 * tensors * piece), bf16),
                pltpu.VMEM((rows, piece), f32),
                pltpu.VMEM((rows, rank), f32),
                pltpu.VMEM((tensors, rows, rank), bf16),
                pltpu.VMEM((rows, tensors * rank), bf16),
                pltpu.VMEM((tensors, rank, width), bf16),
                pltpu.VMEM((2 * tensors, rows, tensors * rank), bf16),
                pltpu.VMEM((chunks, rows, piece), bf16),
                pltpu.VMEM((chunks, sections, rows // sections, piece), bf16),
                pltpu.VMEM((1, rows), jnp.int32),
                pltpu.VMEM((1, adapter_slot.shape[0]), jnp.int32),
                dma((chunks,)),
                dma,
                dma,
                dma,
                dma,
                dma((chunks, 2 * tensors)),
                dma((chunks, tensors)),
                dma((chunks, tensors)),
                dma((chunks, tensors)),
                dma((chunks, tensors)),
                dma((tensors,)),
                dma((tensors,)),
                dma,
                dma((tensors,)),
                dma((tensors,)),
                dma,
                dma((2 * tensors,)),
                dma((2 * tensors,)),
                dma,
                dma,
                dma((tensors,)),
                dma((tensors,)),
                dma((chunks, tensors)),
                dma((chunks, sections)),
                dma((chunks,)),
                dma((chunks,)),
            ],
            compiler_params=pltpu.CompilerParams(
                collective_id=0, has_side_effects=True, vmem_limit_bytes=64 * 1024 * 1024
            ),
        )(
            tokens,
            gain,
            base_weight,
            down,
            up,
            row_adapter.reshape(1, rows),
            adapter_slot.reshape(1, -1),
        )

    return jax.shard_map(
        shards,
        mesh=mesh,
        in_specs=(
            P("parts", ("tensor", "rows")),
            P("section", None),
            P("section", None, ("tensor", "rows")),
            P("section", "tensor", None, "rows"),
            P("section", "tensor", None, "rows"),
            P("parts"),
            P(),
        ),
        out_specs=P(("parts", "section"), ("tensor", "rows")),
        check_vma=False,
    )
```

```python
import functools

import jax
import jax.numpy as jnp
from jax import lax
from jax.experimental import pallas as pl
from jax.experimental.pallas import tpu as pltpu
from jax.sharding import PartitionSpec as P

MESH = pl.DeviceIdType.MESH
epsilon = 1e-05


def crossed(position, offset, count):
    result = position
    bit = 1
    while bit < count:
        if offset & bit:
            result = result + bit - 2 * bit * lax.rem(lax.div(position, bit), 2)
        bit *= 2
    return result


def kernel(
    sections,
    tensors,
    tokens_ref,
    gain_ref,
    weight_ref,
    down_ref,
    up_ref,
    row_ref,
    slot_ref,
    out_ref,
    x_buf,
    w_buf,
    gain_buf,
    down_buf,
    up_buf,
    acc,
    normed,
    squares,
    score,
    low_buf,
    low_all,
    part_down,
    part_score,
    chain_buf,
    out_buf,
    row_buf,
    slot_buf,
    token_sem,
    row_sem,
    slot_sem,
    gain_sem,
    down_sem,
    w_sem,
    x_send,
    x_recv,
    fwd_send,
    fwd_recv,
    up_send,
    up_recv,
    up_local,
    part_down_send,
    part_down_recv,
    part_down_local,
    part_send,
    part_recv,
    down_send,
    down_recv,
    low_send,
    low_recv,
    chain_send,
    out_send,
    out_recv,
    out_local,
):
    s = lax.axis_index("section")
    t = lax.axis_index("tensor")
    h = lax.axis_index("rows")
    other = 1 - h
    chunks, rows, piece = x_buf.shape[0], x_buf.shape[3], x_buf.shape[4]
    width = chunks * piece
    own_chunks = chunks // 2 if sections > 1 else chunks
    me = t * 2 + h
    peers = [crossed(t, j, tensors) for j in range(tensors)]
    pairs = [(j, hh) for j in range(tensors) for hh in range(2)]
    last = sections - 1
    order = sorted(range(chunks), key=lambda c: (c % max(1, chunks // 2), -c))

    def block_of(j, hh):
        return peers[j] * 2 + (h if hh == 0 else other)

    barrier = pltpu.get_barrier_semaphore()

    def greet(device):
        pl.semaphore_signal(barrier, inc=1, device_id=device, device_id_type=MESH)

    for j, hh in pairs:
        if j or hh:
            greet({"tensor": peers[j], "rows": h if hh == 0 else other})
    expected = 2 * tensors - 1
    if sections > 1:

        @pl.when(s > 0)
        def _():
            for j in range(tensors):
                greet({"section": s - 1, "tensor": peers[j]})

        @pl.when(s < last)
        def _():
            for j in range(tensors):
                greet({"section": s + 1, "tensor": peers[j]})

        expected = expected + tensors * (
            jnp.where(s > 0, 1, 0) + jnp.where(s < last, 1, 0)
        )
    if sections > 2:

        @pl.when(s == last)
        def _():
            for d in range(last - 1):
                greet({"section": d})

        @pl.when(s < last - 1)
        def _():
            greet({"section": last})

        expected = (
            expected + jnp.where(s == last, last - 1, 0) + jnp.where(s < last - 1, 1, 0)
        )
    def token_copy(c):
        return pltpu.make_async_copy(
            tokens_ref.at[:, pl.ds(c * piece, piece)], x_buf.at[c, 0, 0], token_sem.at[c]
        )

    @pl.when(s == 0)
    def _():
        for c in range(chunks):
            token_copy(c).start()

    row_copy = pltpu.make_async_copy(row_ref, row_buf, row_sem)
    row_copy.start()
    slot_copy = pltpu.make_async_copy(slot_ref, slot_buf, slot_sem)
    slot_copy.start()
    gain_copy = pltpu.make_async_copy(gain_ref, gain_buf, gain_sem)
    gain_copy.start()
    down_copy = pltpu.make_async_copy(down_ref.at[0, 0], down_buf.at[h], down_sem)

    @pl.when(s == 0)
    def _():
        down_copy.start()

    def w_copy(c, j, hh):
        first = pl.multiple_of(block_of(j, hh) * width + c * piece, piece)
        return pltpu.make_async_copy(
            weight_ref.at[0, pl.ds(first, piece), :],
            w_buf.at[c, pl.ds((2 * j + hh) * piece, piece), :],
            w_sem.at[c, 2 * j + hh],
        )

    for c in range(chunks):
        for j, hh in pairs:
            w_copy(c, j, hh).start()

    pl.semaphore_wait(barrier, expected)

    def token_send(c, j):
        return pltpu.make_async_remote_copy(
            src_ref=tokens_ref.at[:, pl.ds(c * piece, piece)],
            dst_ref=x_buf.at[c, j, 0],
            send_sem=x_send.at[c, j],
            recv_sem=x_recv.at[c, j],
            device_id={"section": 0, "tensor": peers[j]},
            device_id_type=MESH,
        )

    def chain(c, j):
        return pltpu.make_async_remote_copy(
            src_ref=chain_buf.at[c],
            dst_ref=x_buf.at[c, j, 0],
            send_sem=chain_send.at[c, j],
            recv_sem=x_recv.at[c, j],
            device_id={"section": lax.rem(s + 1, sections), "tensor": peers[j]},
            device_id_type=MESH,
        )

    def spread_copy(j):
        return pltpu.make_async_remote_copy(
            src_ref=x_buf.at[0, 0, 0],
            dst_ref=x_buf.at[0, j, 0],
            send_sem=x_send.at[0, j],
            recv_sem=x_recv.at[0, j],
            device_id={"tensor": peers[j]},
            device_id_type=MESH,
        )

    def fwd_copy(c, j):
        return pltpu.make_async_remote_copy(
            src_ref=x_buf.at[c, j, 0],
            dst_ref=x_buf.at[c, j, 1],
            send_sem=fwd_send.at[c, j],
            recv_sem=fwd_recv.at[c, j],
            device_id={"rows": other},
            device_id_type=MESH,
        )

    @pl.when(s == 0)
    def _():
        for c in range(own_chunks):
            for j in range(1, tensors):
                token_send(c, j).start()

    if sections > 1:

        @pl.when(s == 1)
        def _():
            for c in range(own_chunks, chunks):
                for j in range(1, tensors):
                    token_send(c, j).start()

    down_remote = pltpu.make_async_remote_copy(
        src_ref=down_ref.at[0, 0],
        dst_ref=down_buf.at[h],
        send_sem=down_send,
        recv_sem=down_recv,
        device_id={"rows": other},
        device_id_type=MESH,
    )

    @pl.when(s == 0)
    def _():
        down_remote.start()

    def map_remote(i, source, landing, sent, landed):
        dest = h * tensors + i
        return pltpu.make_async_remote_copy(
            src_ref=source.at[0, 0, :, pl.ds(i * width, width)],
            dst_ref=landing.at[t],
            send_sem=sent.at[i],
            recv_sem=landed.at[t],
            device_id={"tensor": lax.div(dest, 2), "rows": lax.rem(dest, 2)},
            device_id_type=MESH,
        )

    def map_here(i, source, landing, done):
        return pltpu.make_async_copy(
            source.at[0, 0, :, pl.ds(i * width, width)], landing.at[t], done
        )

    def send_maps(source, landing, sent, landed, done):
        for i in range(tensors):

            @pl.when(h * tensors + i != me)
            def _():
                map_remote(i, source, landing, sent, landed).start()

            @pl.when(h * tensors + i == me)
            def _():
                map_here(i, source, landing, done).start()

    def wait_maps(source, landing, sent, landed, done):
        half_here = lax.div(me, tensors)
        for k in range(tensors):
            local = (t == k) & (h == half_here)

            @pl.when(local)
            def _():
                map_here(0, source, landing, done).wait()

            @pl.when(jnp.logical_not(local))
            def _():
                pltpu.make_async_remote_copy(
                    src_ref=landing.at[k],
                    dst_ref=landing.at[k],
                    send_sem=sent.at[0],
                    recv_sem=landed.at[k],
                    device_id={"rows": other},
                    device_id_type=MESH,
                ).wait_recv()

    def wait_maps_sent(source, landing, sent, landed, done):
        for i in range(tensors):

            @pl.when(h * tensors + i != me)
            def _():
                map_remote(i, source, landing, sent, landed).wait_send()

    ups = (up_ref, up_buf, up_send, up_recv, up_local)
    downs = (down_ref, part_down, part_down_send, part_down_recv, part_down_local)

    @pl.when(s > 0)
    def _():
        send_maps(*downs)
        send_maps(*ups)

    row_copy.wait()
    slot_copy.wait()
    row = row_buf[...]
    slots = slot_buf[...]
    slot_row = jnp.zeros_like(row)
    for a in range(slots.shape[1]):
        slot_row = jnp.where(row == a, slots[:, a : a + 1], slot_row)
    grid_shape = (rows, rows)
    diagonal = lax.broadcasted_iota(jnp.int32, grid_shape, 0) == lax.broadcasted_iota(
        jnp.int32, grid_shape, 1
    )
    spread = jnp.broadcast_to(slot_row.astype(jnp.float32), grid_shape)
    slot_column = jnp.sum(jnp.where(diagonal, spread, 0.0), axis=1, keepdims=True)
    hot_here = (slot_column == t.astype(jnp.float32)).astype(jnp.float32)
    rank = down_buf.shape[1]

    gain_copy.wait()

    def low_copy(j):
        return pltpu.make_async_remote_copy(
            src_ref=low_buf.at[0],
            dst_ref=low_buf.at[j],
            send_sem=low_send.at[j],
            recv_sem=low_recv.at[j],
            device_id={"tensor": peers[j]},
            device_id_type=MESH,
        )

    def part_copy(j, hh):
        return pltpu.make_async_remote_copy(
            src_ref=part_score.at[0],
            dst_ref=part_score.at[2 * j + hh],
            send_sem=part_send.at[2 * j + hh],
            recv_sem=part_recv.at[2 * j + hh],
            device_id={"tensor": peers[j], "rows": h if hh == 0 else other},
            device_id_type=MESH,
        )

    def absorb(c, j, hh):
        values = x_buf[c, j, hh].astype(jnp.float32)
        if c == 0 and j == 0 and hh == 0:
            squares[...] = values * values
        else:
            squares[...] += values * values
        place = pl.multiple_of(block_of(j, hh) * width + c * piece, piece)
        normed[c, :, (2 * j + hh) * piece : (2 * j + hh + 1) * piece] = (
            values * gain_buf[:, pl.ds(place, piece)]
        ).astype(jnp.bfloat16)

    def multiply(c):
        for j, hh in pairs:
            w_copy(c, j, hh).wait()
        part = jnp.dot(normed[c], w_buf[c], preferred_element_type=jnp.float32)
        acc[...] = part if c == order[0] else acc[...] + part

    for c in range(chunks):

        @pl.when(s == 0)
        def _():
            token_copy(c).wait()

        @pl.when(s > 0)
        def _():
            chain(c, 0).wait_recv()
            if c == 0:
                for j in range(1, tensors):
                    spread_copy(j).start()

        fwd_copy(c, 0).start()
        absorb(c, 0, 0)

    @pl.when(s > 0)
    def _():
        wait_maps(*downs)
        shape = (rows, tensors * rank)
        own = jnp.zeros(shape, jnp.float32)
        for c in range(chunks):
            own = own + lax.dot_general(
                normed[c, :, :piece],
                jnp.concatenate(
                    [part_down[k, :, c * piece : (c + 1) * piece] for k in range(tensors)], axis=0
                ),
                (((1,), (1,)), ((), ())),
                preferred_element_type=jnp.float32,
            )
        slot_of_lane = lax.div(lax.broadcasted_iota(jnp.int32, shape, 1), rank)
        kept = slot_of_lane.astype(jnp.float32) == slot_column
        part_score[0] = jnp.where(kept, own, 0.0).astype(jnp.bfloat16)
        for j, hh in pairs:
            if j or hh:
                part_copy(j, hh).start()

    @pl.when(s == 0)
    def _():
        down_copy.wait()
        down_remote.wait_recv()

    pl.when(s == 0)(lambda: send_maps(*ups))

    for step in range(chunks + 1):
        if step < chunks:
            for j in range(1, tensors):
                chain(order[step], j).wait_recv()
                fwd_copy(order[step], j).start()
        if step == 0:
            continue
        c = order[step - 1]
        for j in range(1, tensors):
            absorb(c, j, 0)
        for j in range(tensors):
            fwd_copy(c, j).wait_recv()
            absorb(c, j, 1)

        @pl.when(s == 0)
        def _():
            down_pieces = []
            for j, hh in pairs:
                block = block_of(j, hh)
                place = pl.multiple_of(lax.rem(block, tensors) * width + c * piece, piece)
                down_pieces.append(down_buf[lax.div(block, tensors), :, pl.ds(place, piece)])
            score_part = lax.dot_general(
                normed[c],
                jnp.concatenate(down_pieces, axis=1),
                (((1,), (1,)), ((), ())),
                preferred_element_type=jnp.float32,
            )
            score[...] = score_part if step == 1 else score[...] + score_part

        if step <= chunks - 1:
            multiply(c)

    mean_square = jnp.sum(squares[...], axis=1, keepdims=True) / (2 * tensors * width)
    scale = lax.rsqrt(mean_square + epsilon)

    @pl.when(s == 0)
    def _():
        low_buf[0] = (hot_here * score[...] * scale).astype(jnp.bfloat16)
        for j in range(1, tensors):
            low_copy(j).start()

    multiply(order[-1])

    wait_maps(*ups)

    @pl.when(s == 0)
    def _():
        for j in range(1, tensors):
            low_copy(j).wait_recv()
        for k in range(tensors):
            low_all[:, k * rank : (k + 1) * rank] = low_buf[peers[k]]

    @pl.when(s > 0)
    def _():
        summed = part_score[0].astype(jnp.float32)
        for j, hh in pairs:
            if j or hh:
                part_copy(j, hh).wait_recv()
                summed = summed + part_score[2 * j + hh].astype(jnp.float32)
        low_all[...] = (summed * scale).astype(jnp.bfloat16)

    share = rows // sections

    def out_copy(c, d):
        return pltpu.make_async_remote_copy(
            src_ref=out_buf.at[c, d],
            dst_ref=out_ref.at[:, pl.ds(c * piece, piece)],
            send_sem=out_send.at[c, d],
            recv_sem=out_recv.at[c],
            device_id={"section": d},
            device_id_type=MESH,
        )

    def out_here(c):
        return pltpu.make_async_copy(
            out_buf.at[c, last], out_ref.at[:, pl.ds(c * piece, piece)], out_local.at[c]
        )

    for c in range(chunks):
        columns = slice(c * piece, (c + 1) * piece)
        update = jnp.dot(
            low_all[...],
            jnp.concatenate([up_buf[k, :, columns] for k in range(tensors)], axis=0),
            preferred_element_type=jnp.float32,
        )
        total = x_buf[c, 0, 0].astype(jnp.float32) + scale * acc[:, columns] + 0.5 * update

        @pl.when(s < last)
        def _():
            chain_buf[c] = total.astype(jnp.bfloat16)
            chain(c, 0).start()

        @pl.when(s == last)
        def _():
            for d in range(sections):
                out_buf[c, d] = total[d * share : (d + 1) * share].astype(jnp.bfloat16)
                if d < last:
                    out_copy(c, d).start()
                else:
                    out_here(c).start()

    @pl.when(s < last)
    def _():
        for c in order:
            if c > 0:
                for j in range(1, tensors):
                    chain(c, j).start()

    @pl.when(s == last)
    def _():
        for c in range(chunks):
            out_here(c).wait()
            for d in range(last):
                out_copy(c, d).wait_send()

    @pl.when(s == 0)
    def _():
        for c in range(own_chunks):
            for j in range(1, tensors):
                token_send(c, j).wait_send()

    if sections > 1:

        @pl.when(s == 1)
        def _():
            for c in range(own_chunks, chunks):
                for j in range(1, tensors):
                    token_send(c, j).wait_send()

    for c in range(chunks):
        for j in range(tensors):
            fwd_copy(c, j).wait_send()
    wait_maps_sent(*ups)

    @pl.when(s == 0)
    def _():
        for j in range(1, tensors):
            low_copy(j).wait_send()
        down_remote.wait_send()

    @pl.when(s > 0)
    def _():
        for j in range(1, tensors):
            spread_copy(j).wait_send()
        wait_maps_sent(*downs)
        for j, hh in pairs:
            if j or hh:
                part_copy(j, hh).wait_send()

    @pl.when(s < last)
    def _():
        for c in range(chunks):
            for j in range(tensors if c > 0 else 1):
                chain(c, j).wait_send()
        for c in range(chunks):
            out_copy(c, 0).wait_recv()


def solution(mesh):
    sections, tensors = mesh.shape["section"], mesh.shape["tensor"]

    def shards(tokens, gain, base_weight, down, up, row_adapter, adapter_slot):
        rows, width = tokens.shape
        features = gain.shape[1]
        rank = down.shape[2]
        piece = max(128, width // 4)
        chunks = width // piece
        bf16, f32 = jnp.bfloat16, jnp.float32
        dma = pltpu.SemaphoreType.DMA
        hbm = pl.BlockSpec(memory_space=pltpu.HBM)
        return pl.pallas_call(
            functools.partial(kernel, sections, tensors),
            out_shape=jax.ShapeDtypeStruct((rows // sections, width), bf16),
            in_specs=[hbm] * 7,
            out_specs=hbm,
            scratch_shapes=[
                pltpu.VMEM((chunks, tensors, 2, rows, piece), bf16),
                pltpu.VMEM((chunks, 2 * tensors * piece, width), bf16),
                pltpu.VMEM((1, features), f32),
                pltpu.VMEM((2, rank, down.shape[3]), bf16),
                pltpu.VMEM((tensors, rank, width), bf16),
                pltpu.VMEM((rows, width), f32),
                pltpu.VMEM((chunks, rows, 2 * tensors * piece), bf16),
                pltpu.VMEM((rows, piece), f32),
                pltpu.VMEM((rows, rank), f32),
                pltpu.VMEM((tensors, rows, rank), bf16),
                pltpu.VMEM((rows, tensors * rank), bf16),
                pltpu.VMEM((tensors, rank, width), bf16),
                pltpu.VMEM((2 * tensors, rows, tensors * rank), bf16),
                pltpu.VMEM((chunks, rows, piece), bf16),
                pltpu.VMEM((chunks, sections, rows // sections, piece), bf16),
                pltpu.VMEM((1, rows), jnp.int32),
                pltpu.VMEM((1, adapter_slot.shape[0]), jnp.int32),
                dma((chunks,)),
                dma,
                dma,
                dma,
                dma,
                dma((chunks, 2 * tensors)),
                dma((chunks, tensors)),
                dma((chunks, tensors)),
                dma((chunks, tensors)),
                dma((chunks, tensors)),
                dma((tensors,)),
                dma((tensors,)),
                dma,
                dma((tensors,)),
                dma((tensors,)),
                dma,
                dma((2 * tensors,)),
                dma((2 * tensors,)),
                dma,
                dma,
                dma((tensors,)),
                dma((tensors,)),
                dma((chunks, tensors)),
                dma((chunks, sections)),
                dma((chunks,)),
                dma((chunks,)),
            ],
            compiler_params=pltpu.CompilerParams(
                collective_id=0, has_side_effects=True, vmem_limit_bytes=64 * 1024 * 1024
            ),
        )(
            tokens,
            gain,
            base_weight,
            down,
            up,
            row_adapter.reshape(1, rows),
            adapter_slot.reshape(1, -1),
        )

    return jax.shard_map(
        shards,
        mesh=mesh,
        in_specs=(
            P("parts", ("tensor", "rows")),
            P("section", None),
            P("section", None, ("tensor", "rows")),
            P("section", "tensor", None, "rows"),
            P("section", "tensor", None, "rows"),
            P("parts"),
            P(),
        ),
        out_specs=P(("parts", "section"), ("tensor", "rows")),
        check_vma=False,
    )
```
